256 devices in a mesh: rep: 4 (over z_lo, core), fsdp: 64 (over z_hi, y, x).
Axes of the slice: x: 4, y: 4, z: 8 (z_hi: 4, z_lo: 2; z = z_hi * 2 + z_lo), core: 2. Of those that a mesh axis runs over, the one named last changes fastest.
Arguments:
- activations: bfloat16 [196608, 8192], P(('rep', 'fsdp')), may hold values from -24 to 24
- cotangents: bfloat16 [196608, 512], P(('rep', 'fsdp')), may hold values from -6 to 6
- momentum: float32 [4, 8192, 512], P('rep', 'fsdp'), may hold values from -6 to 6
Outputs:
- update: float32 [8192, 512], P('fsdp')
- new_momentum: float32 [4, 8192, 512], P('rep', 'fsdp')
The draws below stay inside these ranges and needn't reach their ends.
All inputs are finite; a program needn't handle non-finite values.
Results may differ from the reference program's by a relative error of at most 0.0003.
Values may be sent and summed in bfloat16 or wider, within the bound.
A program may use at most 192 MiB of HBM per device.

```python
import math
import jax
import jax.numpy as jnp
from jax import lax

D = 8192
KW = 512
TOKENS = 196608
N_REP = 4


def raised(drawn, rng, source, target, shards_of, factor):
    owner, partner = [(jnp.arange(drawn.shape[axis_at]) // (drawn.shape[axis_at] // shards_of)).reshape([-1 if axis == axis_at else 1 for axis in range(drawn.ndim)]) for axis_at in (source, target)]
    chosen = jax.random.permutation(rng, shards_of)[partner]
    strong = (owner == chosen) | (owner == (partner + shards_of // 2) % shards_of)
    return jnp.where(strong, factor * drawn, drawn)


def block_scale(key, extent, pieces, smallest, largest):
    def one(dim, blocks):
        steps = jax.random.uniform(jax.random.fold_in(jax.random.fold_in(key, 6), dim), (blocks,), jnp.float32, smallest / len(pieces), largest / len(pieces))
        return jnp.repeat(jnp.exp(steps), extent[dim] // blocks).reshape((-1,) + (1,) * (len(extent) - dim - 1))

    loudness = one(*pieces[0])
    for cut in pieces[1:]:
        loudness = loudness * one(*cut)
    return loudness


def normal_values(key, shape, deviation, limit, cuts=(), kind=jnp.bfloat16):
    gain = block_scale(key, shape, cuts, -0.22, 0.18) if cuts else 1.0
    values = jax.random.normal(key, shape, jnp.float32) * deviation * gain
    return jnp.minimum(jnp.maximum(values, -limit), limit).astype(kind)


def heavy_noise(own_key, dims, scale, limit, cuts, heavy, kind=jnp.bfloat16):
    entries = scale * jax.random.normal(own_key, dims, jnp.float32)
    if cuts:
        entries = entries * block_scale(own_key, dims, cuts, -0.22, 0.18)
    return jnp.clip(raised(entries, jax.random.fold_in(own_key, 3), *heavy), -limit, limit).astype(kind)


def setup_inputs(seed: int = 0) -> dict:
    arg_keys = jax.random.split(jax.random.key(seed), 4)
    activations = heavy_noise(arg_keys[0], (TOKENS, D), 1.0, 24.0, ((0, 256),), (0, 1, 256, 6.0))
    cotangents = normal_values(arg_keys[1], (TOKENS, KW), 1.0, 6.0, ((0, 256),))
    momentum = normal_values(arg_keys[2], (N_REP, D, KW), 1.0, 6.0, ((0, 4), (1, 64)), jnp.float32)
    return dict(activations=activations, cotangents=cotangents, momentum=momentum)


def dct_basis():
    wavenum = jnp.arange(16, dtype=jnp.float32)[:, None]
    sample_pos = jnp.arange(64, dtype=jnp.float32)[None, :]
    factor = jnp.where(wavenum == 0, math.sqrt(1.0 / 64.0), math.sqrt(2.0 / 64.0))
    return (factor * jnp.cos(math.pi * (2.0 * sample_pos + 1.0) * wavenum / 128.0)).astype(jnp.float32)

def band_of(field, basis):
    rows, cols = field.shape
    blocks = field.reshape(rows // 64, 64, cols // 64, 64)
    coeffs = jnp.einsum('fs,asbt,gt->afbg', basis, blocks, basis, precision=lax.Precision.HIGHEST)
    return coeffs.reshape(rows // 4, cols // 4)

def spread_band(band, basis):
    rows, cols = band.shape
    blocks = band.reshape(rows // 16, 16, cols // 16, 16)
    values = jnp.einsum('fs,afbg,gt->asbt', basis, blocks, basis, precision=lax.Precision.HIGHEST)
    return values.reshape(rows * 4, cols * 4)

def reference(activations, cotangents, momentum):
    basis = dct_basis()
    group_tok = activations.shape[0] // momentum.shape[0]
    bands = []
    accums = []
    for group in range(momentum.shape[0]):
        inputs = activations[group * group_tok:(group + 1) * group_tok]
        grads_in = cotangents[group * group_tok:(group + 1) * group_tok]
        gradient = lax.dot_general(inputs, grads_in, (((0,), (0,)), ((), ())), preferred_element_type=jnp.float32)
        gradient = gradient / math.sqrt(group_tok)
        accum = 0.9 * momentum[group] + gradient
        accums.append(accum)
        bands.append(band_of(accum, basis))
    mean_band = lax.optimization_barrier(jnp.mean(jnp.stack(bands), axis=0))
    update = spread_band(mean_band, basis)
    new_momentum = jnp.stack([accums[group] - spread_band(bands[group], basis) for group in range(momentum.shape[0])])
    return (update, new_momentum)
```

```python
import functools
import math

import jax
import jax.numpy as jnp
import numpy as np
from jax import lax
from jax.experimental import pallas as pl
from jax.experimental.pallas import tpu as pltpu
from jax.sharding import PartitionSpec as P

F32 = jnp.float32
BF16 = jnp.bfloat16
FIRST = ((1, 2), (3, 2))
NEXT = (3, 1)
SLABS = (2, 1, 3, 0)
SPAN = 250.0


def dct_basis():
    wavenum = np.arange(16)[:, None]
    sample_pos = np.arange(64)[None, :]
    factor = np.where(wavenum == 0, math.sqrt(1.0 / 64.0), math.sqrt(2.0 / 64.0))
    return (factor * np.cos(math.pi * (2.0 * sample_pos + 1.0) * wavenum / 128.0)).astype(np.float32)


def flip(v, mask):
    return (v // 2 + mask // 2) % 2 * 2 + (v % 2 + mask % 2) % 2


def encode(v):
    size = jnp.abs(v)
    s = jnp.maximum(jnp.max(size, axis=0, keepdims=True), 1e-30)
    code = jnp.exp2(size * (SPAN / s) - SPAN / 2)
    return jnp.where(v < 0, -code, code).astype(BF16), s


def decode(code, s):
    code = code.astype(F32)
    size = jnp.log(jnp.abs(code)) * (s * (1.0 / (SPAN * math.log(2.0)))) + s * 0.5
    return jnp.where(code < 0, -size, size)


def kernel(
    group_tok, a_hbm, c_ref, mom_ref, left_ref, left_t_ref, right_ref, right_t_ref, up_ref, new_ref,
    a, ct, pt, s1, s2, s3, s4, s5, s6, r1, r2, r3, r4, r5, r6, ssc, rsc, band, bands,
    a_sem, ss, rs, sss, rss, band_ss, band_rs,
):
    rep, own = lax.axis_index("rep"), lax.axis_index("fsdp")
    z0, y0, x0 = own // 16, own // 4 % 4, own % 4
    sends, recvs = (s1, s2, s3, s4, s5, s6), (r1, r2, r3, r4, r5, r6)

    def partner(axis, mask):
        z, y, x = z0, y0, x0
        if axis == "x":
            x = flip(x, mask)
        elif axis == "y":
            y = flip(y, mask)
        else:
            z = flip(z, mask)
        return (rep, z * 16 + y * 4 + x)

    def block_copy(q, zh):
        first = pl.multiple_of((zh * 16 + flip(y0, q) * 4) * 128, 512)
        cols = pl.ds(first, 512)
        return pltpu.make_async_copy(a_hbm.at[:, cols], a.at[:, cols], a_sem.at[q, zh])

    for q in SLABS:
        for zh in range(4):
            block_copy(q, zh).start()

    barrier = pltpu.get_barrier_semaphore()
    others = [partner(axis, mask) for axis in "xyz" for mask in (1, 3)]
    others += [((rep + i) % 4, own) for i in (1, 2, 3)]
    for other in others:
        pl.semaphore_signal(barrier, inc=1, device_id=other)
    ct[...] = c_ref[...].T
    pl.semaphore_wait(barrier, len(others))

    def axis_of(f, stage):
        return ("xxzzyy", "yyzzxx")[f][stage]

    def mask_of(p, stage):
        return (FIRST[p][0], NEXT[p])[stage % 2]

    def data(f, p, q, stage, part=None):
        src, dst = sends[stage].at[f, p, q], recvs[stage].at[f, p, q]
        if part is not None:
            src, dst = src.at[part], dst.at[part]
        return pltpu.make_async_remote_copy(
            src, dst, ss.at[f, p, q, stage], rs.at[f, p, q, stage],
            device_id=partner(axis_of(f, stage), mask_of(p, stage)),
        )

    def scales(f, p, q, stage):
        return pltpu.make_async_remote_copy(
            ssc.at[f, p, q, stage], rsc.at[f, p, q, stage], sss.at[f, p, q, stage], rss.at[f, p, q, stage],
            device_id=partner(axis_of(f, stage), mask_of(p, stage)),
        )

    def wait_recv(f, p, q, stage):
        data(f, p, q, stage).wait_recv()
        scales(f, p, q, stage).wait_recv()

    def put(f, p, q, stage, at, row, v):
        code, s = encode(v)
        sends[stage][(f, p, q) + at] = code
        ssc[f, p, q, stage, pl.ds(row, 1), :] = s

    def got(f, p, q, stage, at, row):
        return decode(recvs[stage][(f, p, q) + at], rsc[f, p, q, stage, pl.ds(row, 1), :])

    def rows(p):
        return slice(p * 128, p * 128 + 128)

    def multiply(f, q):
        def one(rz, carry):
            zh = flip(z0, rz)
            parts = []
            for r in range(4):
                y, x = (flip(y0, q), flip(x0, r)) if f == 0 else (flip(y0, r), flip(x0, q))
                parts.append(a[:, pl.ds(pl.multiple_of((zh * 16 + y * 4 + x) * 128, 128), 128)])
            total = jnp.dot(ct[f * 256 : f * 256 + 256, :], jnp.concatenate(parts, axis=1), preferred_element_type=F32)
            for r in range(4):
                pt[f, q, rz, r] = total[:, r * 128 : r * 128 + 128]
            for p in range(2):
                for j, r in enumerate(FIRST[p]):
                    put(f, p, q, 0, (rz, j), rz * 2 + j, pt[f, q, rz, r, rows(p), :])
                data(f, p, q, 0, rz).start()
            return carry

        lax.fori_loop(0, 4, one, 0)
        for p in range(2):
            scales(f, p, q, 0).start()

    def second(f, q):
        for p in range(2):
            wait_recv(f, p, q, 0)

            def one(rz, carry):
                v = pt[f, q, rz, NEXT[p], rows(p), :] + got(f, p, q, 0, (rz, 1), rz * 2 + 1)
                put(f, p, q, 1, (rz,), rz, v)
                data(f, p, q, 1, rz).start()
                pt[f, q, rz, 0, rows(p), :] += got(f, p, q, 0, (rz, 0), rz * 2)
                return carry

            lax.fori_loop(0, 4, one, 0)
            scales(f, p, q, 1).start()

    def third(f, q):
        for p in range(2):
            wait_recv(f, p, q, 1)
            for j, rz in enumerate(FIRST[p]):
                put(f, p, q, 2, (j,), j, pt[f, q, rz, 0, rows(p), :] + got(f, p, q, 1, (rz,), rz))
            data(f, p, q, 2).start()
            scales(f, p, q, 2).start()
            for rz in (0, NEXT[p]):
                pt[f, q, rz, 0, rows(p), :] += got(f, p, q, 1, (rz,), rz)

    def fourth(f, q):
        for p in range(2):
            wait_recv(f, p, q, 2)
            put(f, p, q, 3, (), 0, pt[f, q, NEXT[p], 0, rows(p), :] + got(f, p, q, 2, (1,), 1))
            data(f, p, q, 3).start()
            scales(f, p, q, 3).start()
            pt[f, q, 0, 0, rows(p), :] += got(f, p, q, 2, (0,), 0)

    def fifth(f, q):
        for p in range(2):
            wait_recv(f, p, q, 3)
            v = pt[f, q, 0, 0, rows(p), :] + got(f, p, q, 3, (), 0)
            if q in FIRST[p]:
                j = FIRST[p].index(q)
                put(f, p, j, 4, (), 0, v)
                data(f, p, j, 4).start()
                scales(f, p, j, 4).start()
            else:
                pt[f, q, 0, 0, rows(p), :] = v

    def sixth(f):
        for p in range(2):
            wait_recv(f, p, 1, 4)
            put(f, p, 0, 5, (), 0, pt[f, NEXT[p], 0, 0, rows(p), :] + got(f, p, 1, 4, (), 0))
            data(f, p, 0, 5).start()
            scales(f, p, 0, 5).start()

    def last(f):
        for p in range(2):
            wait_recv(f, p, 0, 4)
            wait_recv(f, p, 0, 5)
            pt[f, 0, 0, 0, rows(p), :] += got(f, p, 0, 4, (), 0) + got(f, p, 0, 5, (), 0)

    steps = [multiply, second, third, fourth, fifth]
    for t in range(4 + len(steps) - 1):
        for k in range(len(steps)):
            if 0 <= t - k < 4:
                for f in range(2):
                    if k == 0 and (f == 0 or t == 0):
                        for q in [SLABS[t]] if f == 0 else SLABS[1:]:
                            if f == 0 and t > 0:
                                continue
                            for zh in range(4):
                                block_copy(q, zh).wait()
                    steps[k](f, SLABS[t - k])
    for f in range(2):
        sixth(f)
    for f in range(2):
        last(f)

    def exact(l, r):
        return jnp.dot(l, r, preferred_element_type=F32, precision=lax.Precision.HIGHEST)

    total = jnp.concatenate([pt[f, 0, 0, 0] for f in range(2)], axis=0)
    accum = 0.9 * mom_ref[0] + total.T * (1.0 / math.sqrt(group_tok))
    mine = exact(exact(left_ref[...], accum), right_ref[...])
    band[...] = mine
    copies = [
        pltpu.make_async_remote_copy(
            band, bands.at[i - 1], band_ss.at[i - 1], band_rs.at[i - 1], device_id=((rep + i) % 4, own)
        )
        for i in (1, 2, 3)
    ]
    for copy in copies:
        copy.start()
    new_ref[0] = accum - exact(exact(left_t_ref[...], mine), right_t_ref[...])
    for copy in copies:
        copy.wait_recv()
    mean = (mine + bands[0] + bands[1] + bands[2]) * 0.25
    up_ref[...] = exact(exact(left_t_ref[...], mean), right_t_ref[...])
    for copy in copies:
        copy.wait_send()
    for f in range(2):
        for p in range(2):
            for stage, slabs in enumerate((4, 4, 4, 4, 2, 1)):
                for q in range(slabs):
                    data(f, p, q, stage).wait_send()
                    scales(f, p, q, stage).wait_send()


def shards(activations, cotangents, momentum):
    tok, d = activations.shape
    kw = cotangents.shape[1]
    basis = dct_basis()
    left = np.kron(np.eye(2, dtype=np.float32), basis)
    right = np.kron(np.eye(kw // 64, dtype=np.float32), basis.T)
    constants = [jnp.asarray(m) for m in (left, left.T.copy(), right, right.T.copy())]
    counts = ((4, 4, 2), (4, 4), (4, 2), (4,), (2,), (1,))
    buffers = [pltpu.VMEM((2, 2) + n + (128, 128), BF16) for n in counts]
    vmem = pl.BlockSpec(memory_space=pltpu.VMEM)
    dma = pltpu.SemaphoreType.DMA
    return pl.pallas_call(
        functools.partial(kernel, tok * lax.axis_size("fsdp")),
        out_shape=(
            jax.ShapeDtypeStruct((128, kw), F32),
            jax.ShapeDtypeStruct((1, 128, kw), F32),
        ),
        in_specs=[pl.BlockSpec(memory_space=pl.ANY)] + [vmem] * 6,
        out_specs=(vmem, vmem),
        scratch_shapes=[
            pltpu.VMEM((tok, d), BF16),
            pltpu.VMEM((kw, tok), BF16),
            pltpu.VMEM((2, 4, 4, 4, 256, 128), F32),
            *buffers,
            *buffers,
            pltpu.VMEM((2, 2, 4, 6, 8, 128), F32),
            pltpu.VMEM((2, 2, 4, 6, 8, 128), F32),
            pltpu.VMEM((32, 128), F32),
            pltpu.VMEM((3, 32, 128), F32),
            dma((4, 4)),
            dma((2, 2, 4, 6)),
            dma((2, 2, 4, 6)),
            dma((2, 2, 4, 6)),
            dma((2, 2, 4, 6)),
            dma((3,)),
            dma((3,)),
        ],
        compiler_params=pltpu.CompilerParams(
            collective_id=0, has_side_effects=True, vmem_limit_bytes=60 * 2**20
        ),
        cost_estimate=pl.CostEstimate(flops=2 * tok * d * kw, bytes_accessed=2 * tok * (d + kw), transcendentals=0),
    )(activations, cotangents, momentum, *constants)


def solution(mesh):
    return jax.shard_map(
        shards,
        mesh=mesh,
        in_specs=(P(("rep", "fsdp"), None), P(("rep", "fsdp"), None), P("rep", "fsdp", None)),
        out_specs=(P("fsdp", None), P("rep", "fsdp", None)),
        check_vma=False,
    )
```

```python
import functools
import math

import jax
import jax.numpy as jnp
import numpy as np
from jax import lax
from jax.experimental import pallas as pl
from jax.experimental.pallas import tpu as pltpu
from jax.sharding import PartitionSpec as P

F32 = jnp.float32
BF16 = jnp.bfloat16
FIRST = ((1, 2), (3, 2))
NEXT = (3, 1)
SLABS = (2, 1, 3, 0)
UNITS = (8, 4, 2, 1, 1, 1)
COUNTS = (4, 4, 4, 4, 2, 1)
SIZES = tuple(n * 128 + 16 for n in UNITS)
STARTS = tuple(sum(n * m for n, m in zip(SIZES[:i], COUNTS)) for i in range(7))
SPAN = 250.0


def dct_basis():
    wavenum = np.arange(16)[:, None]
    sample_pos = np.arange(64)[None, :]
    factor = np.where(wavenum == 0, math.sqrt(1.0 / 64.0), math.sqrt(2.0 / 64.0))
    return (factor * np.cos(math.pi * (2.0 * sample_pos + 1.0) * wavenum / 128.0)).astype(np.float32)


def flip(v, mask):
    return (v // 2 + mask // 2) % 2 * 2 + (v % 2 + mask % 2) % 2


def encode(v):
    size = jnp.abs(v)
    s = jnp.maximum(jnp.max(size, axis=0, keepdims=True), 1e-30)
    s = (s * 1.004).astype(BF16).astype(F32)
    code = jnp.exp2(size * (SPAN / s) - SPAN / 2)
    return jnp.where(v < 0, -code, code).astype(BF16), s


def decode(code, s):
    code = code.astype(F32)
    size = jnp.log(jnp.abs(code)) * (s * (1.0 / (SPAN * math.log(2.0)))) + s * 0.5
    return jnp.where(code < 0, -size, size)


def kernel(
    group_tok, a_hbm, c_hbm, mom_hbm, left_hbm, left_t_hbm, right_hbm, right_t_hbm, up_hbm, new_hbm,
    a, c, ct, mom, left, left_t, right, right_t, pt, sent, received, ssc, rsc, up, new, band, bands,
    a_sem, in_sem, out_sem, sent_sem, rs, band_ss, band_rs,
):
    rep, own = lax.axis_index("rep"), lax.axis_index("fsdp")
    z0, y0, x0 = own // 16, own // 4 % 4, own % 4

    def partner(axis, mask):
        z, y, x = z0, y0, x0
        if axis == "x":
            x = flip(x, mask)
        elif axis == "y":
            y = flip(y, mask)
        else:
            z = flip(z, mask)
        return (rep, z * 16 + y * 4 + x)

    def slab(t):
        return (t + 1) % 2 * 2 + (t + 1) // 2 % 2

    def block_copy(t, ry):
        first = pl.multiple_of((flip(z0, slab(t)) * 16 + flip(y0, ry) * 4) * 128, 512)
        cols = pl.ds(first, 512)
        return pltpu.make_async_copy(a_hbm.at[:, cols], a.at[:, cols], a_sem.at[t, ry])

    barrier = pltpu.get_barrier_semaphore()
    others = [partner(axis, mask) for axis in "xyz" for mask in (1, 3)]
    others += [((rep + i) % 4, own) for i in (1, 2, 3)]
    for other in others:
        pl.semaphore_signal(barrier, inc=1, device_id=other)
    pairs = [(c_hbm, c), (mom_hbm, mom), (left_hbm, left), (left_t_hbm, left_t), (right_hbm, right), (right_t_hbm, right_t)]
    inputs = [pltpu.make_async_copy(src, dst, in_sem.at[i]) for i, (src, dst) in enumerate(pairs)]
    inputs[0].start()
    for t in range(4):
        for ry in SLABS:
            block_copy(t, ry).start()
    for copy in inputs[1:]:
        copy.start()
    inputs[0].wait()
    ct[...] = c[...].T
    ssc[...] = jnp.zeros_like(ssc)

    def axis_of(f, stage):
        return ("xxyyzz", "yyxxzz")[f][stage]

    def mask_of(p, stage):
        return (FIRST[p][0], NEXT[p])[stage % 2]

    def begin(f, p, t, stage, row=0):
        at = (f * 2 + p) * STARTS[6] + STARTS[stage] + t * SIZES[stage] + row
        return at if isinstance(at, int) else pl.multiple_of(at, 16)

    def message(f, p, t, stage):
        where = pl.ds(begin(f, p, t, stage), SIZES[stage])
        return pltpu.make_async_remote_copy(
            sent.at[where], received.at[where], sent_sem.at[0], rs.at[f, p, t, stage],
            device_id=partner(axis_of(f, stage), mask_of(p, stage)),
        )

    def put(f, p, t, stage, row, v):
        code, s = encode(v)
        sent[pl.ds(begin(f, p, t, stage, row * 128), 128), :] = code
        ssc[f, p, pl.ds(row, 1), :] = s

    def send(f, p, t, stage):
        sent[pl.ds(begin(f, p, t, stage, UNITS[stage] * 128), 16), :] = ssc[f, p].astype(BF16)
        message(f, p, t, stage).start()

    def receive(f, p, t, stage):
        message(f, p, t, stage).wait_recv()
        rsc[f, p] = received[pl.ds(begin(f, p, t, stage, UNITS[stage] * 128), 16), :].astype(F32)

    def got(f, p, t, stage, row):
        return decode(received[pl.ds(begin(f, p, t, stage, row * 128), 128), :], rsc[f, p, pl.ds(row, 1), :])

    def unit(f, p, t, sec, pri):
        at = (sec, pri) if f == 0 else (pri, sec)
        return (t,) + at + (slice((f * 2 + p) * 128, (f * 2 + p) * 128 + 128), slice(None))

    def multiply(t, ry):
        zh = flip(z0, slab(t))
        block_copy(t, ry).wait()
        parts = []
        for rx in range(4):
            col = (zh * 16 + flip(y0, ry) * 4 + flip(x0, rx)) * 128
            parts.append(a[:, pl.ds(pl.multiple_of(col, 128), 128)])
        total = jnp.dot(ct[...], jnp.concatenate(parts, axis=1), preferred_element_type=F32)
        for rx in range(4):
            pt[t, ry, rx] = total[:, rx * 128 : rx * 128 + 128]

    def first(t):
        for ry in SLABS:
            multiply(t, ry)
            for p in range(2):
                for j, rx in enumerate(FIRST[p]):
                    put(0, p, t, 0, j * 4 + ry, pt[unit(0, p, t, ry, rx)])
            for p in range(2):
                if ry in FIRST[p]:
                    for rx in range(4):
                        put(1, p, t, 0, FIRST[p].index(ry) * 4 + rx, pt[unit(1, p, t, rx, ry)])
            if ry == 1:

                @pl.when(t == 0)
                def _():
                    pl.semaphore_wait(barrier, len(others))

                send(1, 0, t, 0)
            if ry == 3:
                send(1, 1, t, 0)
        send(0, 0, t, 0)
        send(0, 1, t, 0)

    def second(t):
        for f in (1, 0):
            for p in range(2):
                receive(f, p, t, 0)

                def one(sec, carry):
                    put(f, p, t, 1, sec, pt[unit(f, p, t, sec, NEXT[p])] + got(f, p, t, 0, 4 + sec))
                    pt[unit(f, p, t, sec, 0)] += got(f, p, t, 0, sec)
                    return carry

                lax.fori_loop(0, 4, one, 0)
                send(f, p, t, 1)

    def third(t):
        for f in (1, 0):
            for p in range(2):
                receive(f, p, t, 1)
                for j, sec in enumerate(FIRST[p]):
                    put(f, p, t, 2, j, pt[unit(f, p, t, sec, 0)] + got(f, p, t, 1, sec))
                send(f, p, t, 2)
                for sec in (0, NEXT[p]):
                    pt[unit(f, p, t, sec, 0)] += got(f, p, t, 1, sec)

    def fourth(t):
        for f in (1, 0):
            for p in range(2):
                receive(f, p, t, 2)
                put(f, p, t, 3, 0, pt[unit(f, p, t, NEXT[p], 0)] + got(f, p, t, 2, 1))
                send(f, p, t, 3)
                pt[unit(f, p, t, 0, 0)] += got(f, p, t, 2, 0)

    def fifth(t):
        for f in (1, 0):
            for p in range(2):
                receive(f, p, t, 3)
                pt[unit(f, p, t, 0, 0)] += got(f, p, t, 3, 0)
                for j, q in enumerate(FIRST[p]):

                    @pl.when(t == SLABS.index(q))
                    def _():
                        put(f, p, j, 4, 0, pt[unit(f, p, t, 0, 0)])
                        send(f, p, j, 4)

    def sixth():
        for f in (1, 0):
            for p in range(2):
                receive(f, p, 1, 4)
                put(f, p, 0, 5, 0, pt[unit(f, p, SLABS.index(NEXT[p]), 0, 0)] + got(f, p, 1, 4, 0))
                send(f, p, 0, 5)

    def last():
        for f in (1, 0):
            for p in range(2):
                for stage in (4, 5):
                    receive(f, p, 0, stage)
                    pt[unit(f, p, 3, 0, 0)] += got(f, p, 0, stage, 0)

    def step(t, carry):
        for k, stage in enumerate((first, second, third, fourth, fifth)):

            @pl.when(jnp.logical_and(t >= k, t < k + 4))
            def _():
                stage(t - k)

        @pl.when(t == 6)
        def _():
            sixth()

        return carry

    lax.fori_loop(0, 8, step, 0)
    last()
    for copy in inputs[1:]:
        copy.wait()

    def exact(l, r):
        return jnp.dot(l, r, preferred_element_type=F32, precision=lax.Precision.HIGHEST)

    accum = 0.9 * mom[0] + pt[3, 0, 0].T * (1.0 / math.sqrt(group_tok))
    mine = exact(exact(left[...], accum), right[...])
    band[...] = mine
    copies = [
        pltpu.make_async_remote_copy(
            band, bands.at[i - 1], band_ss.at[i - 1], band_rs.at[i - 1], device_id=((rep + i) % 4, own)
        )
        for i in (1, 2, 3)
    ]
    for copy in copies:
        copy.start()
    new[0] = accum - exact(exact(left_t[...], mine), right_t[...])
    outs = [pltpu.make_async_copy(*refs, out_sem.at[i]) for i, refs in enumerate(((up, up_hbm), (new, new_hbm)))]
    outs[1].start()
    for copy in copies:
        copy.wait_recv()
    mean = (mine + bands[0] + bands[1] + bands[2]) * 0.25
    up[...] = exact(exact(left_t[...], mean), right_t[...])
    outs[0].start()
    for copy in copies:
        copy.wait_send()
    pltpu.make_async_copy(sent, sent, sent_sem.at[0]).wait()
    for copy in outs:
        copy.wait()


def hand_on(up_ref, new_ref, up_out, new_out):
    up_out[...] = up_ref[...]
    new_out[...] = new_ref[...]


def shards(activations, cotangents, momentum):
    tok, d = activations.shape
    kw = cotangents.shape[1]
    basis = dct_basis()
    left = np.kron(np.eye(2, dtype=np.float32), basis)
    right = np.kron(np.eye(kw // 64, dtype=np.float32), basis.T)
    constants = [jnp.asarray(m) for m in (left, left.T.copy(), right, right.T.copy())]
    vmem = pl.BlockSpec(memory_space=pltpu.VMEM)
    hbm = pl.BlockSpec(memory_space=pl.ANY)
    dma = pltpu.SemaphoreType.DMA
    shapes = (jax.ShapeDtypeStruct((128, kw), F32), jax.ShapeDtypeStruct((1, 128, kw), F32))
    results = pl.pallas_call(
        functools.partial(kernel, tok * lax.axis_size("fsdp")),
        out_shape=shapes,
        in_specs=[hbm] * 7,
        out_specs=(hbm, hbm),
        scratch_shapes=[
            pltpu.VMEM((tok, d), BF16),
            pltpu.VMEM((tok, kw), BF16),
            pltpu.VMEM((kw, tok), BF16),
            pltpu.VMEM((1, 128, kw), F32),
            *[pltpu.VMEM(m.shape, F32) for m in constants],
            pltpu.VMEM((4, 4, 4, kw, 128), F32),
            pltpu.VMEM((4 * STARTS[6], 128), BF16),
            pltpu.VMEM((4 * STARTS[6], 128), BF16),
            pltpu.VMEM((2, 2, 16, 128), F32),
            pltpu.VMEM((2, 2, 16, 128), F32),
            *[pltpu.VMEM(m.shape, F32) for m in shapes],
            pltpu.VMEM((32, 128), F32),
            pltpu.VMEM((3, 32, 128), F32),
            dma((4, 4)),
            dma((6,)),
            dma((2,)),
            dma((1,)),
            dma((2, 2, 4, 6)),
            dma((3,)),
            dma((3,)),
        ],
        compiler_params=pltpu.CompilerParams(
            collective_id=0, has_side_effects=True, vmem_limit_bytes=60 * 2**20
        ),
        cost_estimate=pl.CostEstimate(flops=2 * tok * d * kw, bytes_accessed=2 * tok * (d + kw), transcendentals=0),
    )(activations, cotangents, momentum, *constants)
    return pl.pallas_call(
        hand_on,
        out_shape=shapes,
        in_specs=[vmem] * 2,
        out_specs=(vmem, vmem),
    )(*results)


def solution(mesh):
    return jax.shard_map(
        shards,
        mesh=mesh,
        in_specs=(P(("rep", "fsdp"), None), P(("rep", "fsdp"), None), P("rep", "fsdp", None)),
        out_specs=(P("fsdp", None), P("rep", "fsdp", None)),
        check_vma=False,
    )
```

```python
import functools
import math

import jax
import jax.numpy as jnp
import numpy as np
from jax import lax
from jax.experimental import pallas as pl
from jax.experimental.pallas import tpu as pltpu
from jax.sharding import PartitionSpec as P

F32 = jnp.float32
BF16 = jnp.bfloat16
FIRST = ((1, 2), (3, 2))
NEXT = (3, 1)
SLABS = (2, 1, 3, 0)
PORTIONS = ((1, 0), (1, 1), (0, 0), (0, 1))
DEPTH = (112, 112, 32)
UNITS = ((8, 4, 2, 1, 1, 1),) * 2 + ((8, 4, 4, 1),)
COUNTS = ((4, 4, 2, 2, 3, 6),) * 2 + ((4, 4, 3, 3),)
SIZES = tuple(tuple(n * depth + 16 for n in units) for depth, units in zip(DEPTH, UNITS))
STARTS = tuple(
    tuple(sum(n * m for n, m in zip(sizes[:i], counts)) for i in range(len(sizes) + 1))
    for sizes, counts in zip(SIZES, COUNTS)
)
FAMILIES = tuple(2 * sum(starts[-1] for starts in STARTS[:i]) for i in range(4))
SPAN = 250.0


def dct_basis():
    wavenum = np.arange(16)[:, None]
    sample_pos = np.arange(64)[None, :]
    factor = np.where(wavenum == 0, math.sqrt(1.0 / 64.0), math.sqrt(2.0 / 64.0))
    return (factor * np.cos(math.pi * (2.0 * sample_pos + 1.0) * wavenum / 128.0)).astype(np.float32)


def flip(v, mask):
    return (v // 2 + mask // 2) % 2 * 2 + (v % 2 + mask % 2) % 2


def encode(v):
    size = jnp.abs(v)
    s = jnp.maximum(jnp.max(size, axis=0, keepdims=True), 1e-30)
    s = (s * 1.004).astype(BF16).astype(F32)
    code = jnp.exp2(size * (SPAN / s) - SPAN / 2)
    return jnp.where(v < 0, -code, code).astype(BF16), s


def decode(code, s):
    code = code.astype(F32)
    size = jnp.log(jnp.abs(code)) * (s * (1.0 / (SPAN * math.log(2.0)))) + s * 0.5
    return jnp.where(code < 0, -size, size)


def kernel(
    group_tok, a_hbm, c_hbm, mom_hbm, left_hbm, left_t_hbm, right_hbm, right_t_hbm, up_hbm, new_hbm,
    a, c, ct, mom, left, left_t, right, right_t, pt, sent, received, ssc, rsc, up, new, band, bands,
    a_sem, in_sem, out_sem, sent_sem, rs, band_ss, band_rs,
):
    rep, own = lax.axis_index("rep"), lax.axis_index("fsdp")
    z0, y0, x0 = own // 16, own // 4 % 4, own % 4

    def partner(axis, mask):
        z, y, x = z0, y0, x0
        if axis == "x":
            x = flip(x, mask)
        elif axis == "y":
            y = flip(y, mask)
        else:
            z = flip(z, mask)
        return (rep, z * 16 + y * 4 + x)

    def slab(t):
        return (t + 1) % 2 * 2 + (t + 1) // 2 % 2

    def block_copy(t, ry):
        first = pl.multiple_of((flip(z0, slab(t)) * 16 + flip(y0, ry) * 4) * 128, 512)
        cols = pl.ds(first, 512)
        return pltpu.make_async_copy(a_hbm.at[:, cols], a.at[:, cols], a_sem.at[t, ry])

    barrier = pltpu.get_barrier_semaphore()
    others = [partner(axis, mask) for axis in "xyz" for mask in (1, 2, 3)]
    others += [((rep + i) % 4, own) for i in (1, 2, 3)]
    for other in others:
        pl.semaphore_signal(barrier, inc=1, device_id=other)
    pairs = [(c_hbm, c), (mom_hbm, mom), (left_hbm, left), (left_t_hbm, left_t), (right_hbm, right), (right_t_hbm, right_t)]
    inputs = [pltpu.make_async_copy(src, dst, in_sem.at[i]) for i, (src, dst) in enumerate(pairs)]
    inputs[0].start()
    for t in range(4):
        for ry in SLABS:
            block_copy(t, ry).start()
    for copy in inputs[1:]:
        copy.start()
    inputs[0].wait()
    ct[...] = c[...].T
    ssc[...] = jnp.zeros_like(ssc)

    def axis_of(f, p, stage):
        return ("zzxy", "zzyx")[p][stage] if f == 2 else ("xxyyzy", "yyxxzx")[f][stage]

    def mask_of(p, stage):
        return (FIRST[p][0], NEXT[p])[stage % 2]

    def begin(f, p, t, stage, row=0):
        at = FAMILIES[f] + p * STARTS[f][-1] + STARTS[f][stage] + t * SIZES[f][stage] + row
        return at if isinstance(at, int) else pl.multiple_of(at, 16)

    def message(f, p, t, stage, mask=None):
        where = pl.ds(begin(f, p, t, stage), SIZES[f][stage])
        return pltpu.make_async_remote_copy(
            sent.at[where], received.at[where], sent_sem.at[0], rs.at[f, p, t, stage],
            device_id=partner(axis_of(f, p, stage), mask or mask_of(p, stage)),
        )

    def put(f, p, t, stage, row, v):
        code, s = encode(v)
        sent[pl.ds(begin(f, p, t, stage, row * DEPTH[f]), DEPTH[f]), :] = code
        ssc[f, p, pl.ds(row, 1), :] = s

    def send(f, p, t, stage, mask=None):
        sent[pl.ds(begin(f, p, t, stage, UNITS[f][stage] * DEPTH[f]), 16), :] = ssc[f, p].astype(BF16)
        message(f, p, t, stage, mask).start()

    def receive(f, p, t, stage):
        message(f, p, t, stage).wait_recv()
        rsc[f, p] = received[pl.ds(begin(f, p, t, stage, UNITS[f][stage] * DEPTH[f]), 16), :].astype(F32)

    def got(f, p, t, stage, row):
        return decode(received[pl.ds(begin(f, p, t, stage, row * DEPTH[f]), DEPTH[f]), :], rsc[f, p, pl.ds(row, 1), :])

    def unit(f, p, t, sec, pri):
        at = (sec, pri) if f == 0 else (pri, sec)
        return (t,) + at + (slice((f * 2 + p) * 112, (f * 2 + p) * 112 + 112), slice(None))

    def multiply(t, ry):
        zh = flip(z0, slab(t))
        block_copy(t, ry).wait()
        parts = []
        for rx in range(4):
            col = (zh * 16 + flip(y0, ry) * 4 + flip(x0, rx)) * 128
            parts.append(a[:, pl.ds(pl.multiple_of(col, 128), 128)])
        total = jnp.dot(ct[...], jnp.concatenate(parts, axis=1), preferred_element_type=F32)
        for rx in range(4):
            pt[t, ry, rx] = total[:, rx * 128 : rx * 128 + 128]

    def z_unit(p, rz, ry, rx):
        return (SLABS.index(rz), ry, rx, slice(448 + p * 32, 480 + p * 32), slice(None))

    def products(t):
        for ry in SLABS:
            multiply(t, ry)

    def first(t):
        @pl.when(t == 0)
        def _():
            pl.semaphore_wait(barrier, len(others))

        for f, p in PORTIONS:
            for j, pri in enumerate(FIRST[p]):
                for sec in range(4):
                    put(f, p, t, 0, j * 4 + sec, pt[unit(f, p, t, sec, pri)])
            send(f, p, t, 0)

    def z_first():
        for p in range(2):

            def one(ry, carry):
                for j, rz in enumerate(FIRST[p]):
                    for rx in range(4):
                        put(2, p, ry, 0, j * 4 + rx, pt[z_unit(p, rz, ry, rx)])
                send(2, p, ry, 0)
                return carry

            lax.fori_loop(0, 4, one, 0)

    def z_second():
        for p in range(2):

            def one(ry, carry):
                receive(2, p, ry, 0)
                for rx in range(4):
                    put(2, p, ry, 1, rx, pt[z_unit(p, NEXT[p], ry, rx)] + got(2, p, ry, 0, 4 + rx))
                send(2, p, ry, 1)
                for rx in range(4):
                    pt[z_unit(p, 0, ry, rx)] += got(2, p, ry, 0, rx)
                return carry

            lax.fori_loop(0, 4, one, 0)

    def z_third():
        for p in range(2):

            def one(ry, carry):
                receive(2, p, ry, 1)
                for rx in range(4):
                    pt[z_unit(p, 0, ry, rx)] += got(2, p, ry, 1, rx)
                return carry

            lax.fori_loop(0, 4, one, 0)
            for m in (2, 1, 3):
                for other in range(4):
                    ry, rx = (other, m) if p == 0 else (m, other)
                    put(2, p, m - 1, 2, other, pt[z_unit(p, 0, ry, rx)])
                send(2, p, m - 1, 2, m)

    def z_fourth():
        for p in range(2):
            for m in (1, 3, 2):
                receive(2, p, m - 1, 2)
                for other in range(4):
                    ry, rx = (other, 0) if p == 0 else (0, other)
                    pt[z_unit(p, 0, ry, rx)] += got(2, p, m - 1, 2, other)
            for m in (2, 1, 3):
                ry, rx = (m, 0) if p == 0 else (0, m)
                put(2, p, m - 1, 3, 0, pt[z_unit(p, 0, ry, rx)])
                send(2, p, m - 1, 3, m)

    def z_last():
        for p in range(2):
            for m in (1, 3, 2):
                receive(2, p, m - 1, 3)
                pt[z_unit(p, 0, 0, 0)] += got(2, p, m - 1, 3, 0)

    def second(t):
        for f, p in PORTIONS:
            receive(f, p, t, 0)

            def pass_on(sec, carry):
                put(f, p, t, 1, sec, pt[unit(f, p, t, sec, NEXT[p])] + got(f, p, t, 0, 4 + sec))
                return carry

            lax.fori_loop(0, 4, pass_on, 0)
            send(f, p, t, 1)
        for f, p in PORTIONS:

            def keep(sec, carry):
                pt[unit(f, p, t, sec, 0)] += got(f, p, t, 0, sec)
                return carry

            lax.fori_loop(0, 4, keep, 0)

    def third_pairs(t):
        for f, p in PORTIONS:
            receive(f, p, t, 1)
            for j, sec in enumerate(FIRST[p]):
                put(f, p, t, 2, j, pt[unit(f, p, t, sec, 0)] + got(f, p, t, 1, sec))
            send(f, p, t, 2)
        for f, p in PORTIONS:
            for sec in (0, NEXT[p]):
                pt[unit(f, p, t, sec, 0)] += got(f, p, t, 1, sec)

    def third_direct(t):
        for f, p in PORTIONS:
            receive(f, p, t, 1)
            for m in (2, 1, 3):
                slot = (t - 2) * 3 + m - 1
                put(f, p, slot, 5, 0, pt[unit(f, p, t, m, 0)] + got(f, p, t, 1, m))
                send(f, p, slot, 5, m)
        for f, p in PORTIONS:
            pt[unit(f, p, t, 0, 0)] += got(f, p, t, 1, 0)

    def fourth_pairs(t):
        for f, p in PORTIONS:
            receive(f, p, t, 2)
            put(f, p, t, 3, 0, pt[unit(f, p, t, NEXT[p], 0)] + got(f, p, t, 2, 1))
            send(f, p, t, 3)
        for f, p in PORTIONS:
            pt[unit(f, p, t, 0, 0)] += got(f, p, t, 2, 0)

    def fourth_direct(t):
        for f, p in PORTIONS:
            v = pt[unit(f, p, t, 0, 0)]
            for m in (1, 3, 2):
                slot = (t - 2) * 3 + m - 1
                receive(f, p, slot, 5)
                v += got(f, p, slot, 5, 0)
            pt[unit(f, p, t, 0, 0)] = v

            @pl.when(t == 2)
            def _():
                put(f, p, 2, 4, 0, pt[unit(f, p, t, 0, 0)])
                send(f, p, 2, 4, 3)

    def fifth(t):
        for f, p in PORTIONS:
            receive(f, p, t, 3)
            pt[unit(f, p, t, 0, 0)] += got(f, p, t, 3, 0)
            for q in (2, 1):

                @pl.when(t == SLABS.index(q))
                def _():
                    put(f, p, q - 1, 4, 0, pt[unit(f, p, t, 0, 0)])
                    send(f, p, q - 1, 4, q)

    def last(q):
        for f, p in PORTIONS:
            receive(f, p, q - 1, 4)
            pt[unit(f, p, 3, 0, 0)] += got(f, p, q - 1, 4, 0)

    def at(when, stage, t):
        pl.when(when)(lambda: stage(t))

    def step(t, carry):
        at(t < 4, first, t)
        at(t < 3, products, t + 1)
        pl.when(t == 2)(z_first)
        at(jnp.logical_and(t >= 1, t < 5), second, t - 1)
        at(jnp.logical_and(t >= 2, t < 4), third_pairs, t - 2)
        at(t >= 4, third_direct, t - 2)
        at(jnp.logical_and(t >= 3, t < 5), fourth_pairs, t - 3)
        pl.when(t == 3)(z_second)
        pl.when(t == 4)(z_third)
        pl.when(t == 5)(z_fourth)
        at(t >= 5, fourth_direct, t - 3)
        at(t >= 4, fifth, t - 4)
        return carry

    products(0)
    lax.fori_loop(0, 6, step, 0)
    last(2)
    last(1)
    fourth_direct(3)
    z_last()
    last(3)
    for copy in inputs[1:]:
        copy.wait()

    def exact(l, r):
        return jnp.dot(l, r, preferred_element_type=F32, precision=lax.Precision.HIGHEST)

    accum = 0.9 * mom[0] + pt[3, 0, 0].T * (1.0 / math.sqrt(group_tok))
    mine = exact(exact(left[...], accum), right[...])
    band[...] = mine
    copies = [
        pltpu.make_async_remote_copy(
            band, bands.at[i - 1], band_ss.at[i - 1], band_rs.at[i - 1], device_id=((rep + i) % 4, own)
        )
        for i in (1, 2, 3)
    ]
    for copy in copies:
        copy.start()
    new[0] = accum - exact(exact(left_t[...], mine), right_t[...])
    outs = [pltpu.make_async_copy(*refs, out_sem.at[i]) for i, refs in enumerate(((up, up_hbm), (new, new_hbm)))]
    outs[1].start()
    for copy in copies:
        copy.wait_recv()
    mean = (mine + bands[0] + bands[1] + bands[2]) * 0.25
    up[...] = exact(exact(left_t[...], mean), right_t[...])
    outs[0].start()
    for copy in copies:
        copy.wait_send()
    pltpu.make_async_copy(sent, sent, sent_sem.at[0]).wait()
    for copy in outs:
        copy.wait()


def hand_on(up_ref, new_ref, up_out, new_out):
    up_out[...] = up_ref[...]
    new_out[...] = new_ref[...]


def shards(activations, cotangents, momentum):
    tok, d = activations.shape
    kw = cotangents.shape[1]
    basis = dct_basis()
    left = np.kron(np.eye(2, dtype=np.float32), basis)
    right = np.kron(np.eye(kw // 64, dtype=np.float32), basis.T)
    constants = [jnp.asarray(m) for m in (left, left.T.copy(), right, right.T.copy())]
    vmem = pl.BlockSpec(memory_space=pltpu.VMEM)
    hbm = pl.BlockSpec(memory_space=pl.ANY)
    dma = pltpu.SemaphoreType.DMA
    shapes = (jax.ShapeDtypeStruct((128, kw), F32), jax.ShapeDtypeStruct((1, 128, kw), F32))
    results = pl.pallas_call(
        functools.partial(kernel, tok * lax.axis_size("fsdp")),
        out_shape=shapes,
        in_specs=[hbm] * 7,
        out_specs=(hbm, hbm),
        scratch_shapes=[
            pltpu.VMEM((tok, d), BF16),
            pltpu.VMEM((tok, kw), BF16),
            pltpu.VMEM((kw, tok), BF16),
            pltpu.VMEM((1, 128, kw), F32),
            *[pltpu.VMEM(m.shape, F32) for m in constants],
            pltpu.VMEM((4, 4, 4, kw, 128), F32),
            pltpu.VMEM((FAMILIES[3], 128), BF16),
            pltpu.VMEM((FAMILIES[3], 128), BF16),
            pltpu.VMEM((3, 2, 16, 128), F32),
            pltpu.VMEM((3, 2, 16, 128), F32),
            *[pltpu.VMEM(m.shape, F32) for m in shapes],
            pltpu.VMEM((32, 128), F32),
            pltpu.VMEM((3, 32, 128), F32),
            dma((4, 4)),
            dma((6,)),
            dma((2,)),
            dma((1,)),
            dma((3, 2, 6, 6)),
            dma((3,)),
            dma((3,)),
        ],
        compiler_params=pltpu.CompilerParams(
            collective_id=0, has_side_effects=True, vmem_limit_bytes=60 * 2**20
        ),
        cost_estimate=pl.CostEstimate(flops=2 * tok * d * kw, bytes_accessed=2 * tok * (d + kw), transcendentals=0),
    )(activations, cotangents, momentum, *constants)
    return pl.pallas_call(
        hand_on,
        out_shape=shapes,
        in_specs=[vmem] * 2,
        out_specs=(vmem, vmem),
    )(*results)


def solution(mesh):
    return jax.shard_map(
        shards,
        mesh=mesh,
        in_specs=(P(("rep", "fsdp"), None), P(("rep", "fsdp"), None), P("rep", "fsdp", None)),
        out_specs=(P("fsdp", None), P("rep", "fsdp", None)),
        check_vma=False,
    )
```

```python
import functools
import math

import jax
import jax.numpy as jnp
import numpy as np
from jax import lax
from jax.experimental import pallas as pl
from jax.experimental.pallas import tpu as pltpu
from jax.sharding import PartitionSpec as P

F32 = jnp.float32
BF16 = jnp.bfloat16
FIRST = ((1, 2), (3, 2))
NEXT = (3, 1)
SLABS = (2, 1, 3, 0)
PORTIONS = ((1, 0), (1, 1), (0, 0), (0, 1))
DEPTH = (112, 112, 32)
UNITS = ((8, 4, 2, 1, 1, 1),) * 2 + ((8, 4, 4, 1),)
COUNTS = ((4, 4, 2, 2, 3, 6),) * 2 + ((4, 4, 3, 3),)
SIZES = tuple(tuple(n * depth + 16 for n in units) for depth, units in zip(DEPTH, UNITS))
STARTS = tuple(
    tuple(sum(n * m for n, m in zip(sizes[:i], counts)) for i in range(len(sizes) + 1))
    for sizes, counts in zip(SIZES, COUNTS)
)
FAMILIES = tuple(2 * sum(starts[-1] for starts in STARTS[:i]) for i in range(4))
SPAN = 250.0


def dct_basis():
    wavenum = np.arange(16)[:, None]
    sample_pos = np.arange(64)[None, :]
    factor = np.where(wavenum == 0, math.sqrt(1.0 / 64.0), math.sqrt(2.0 / 64.0))
    return (factor * np.cos(math.pi * (2.0 * sample_pos + 1.0) * wavenum / 128.0)).astype(np.float32)


def flip(v, mask):
    return (v // 2 + mask // 2) % 2 * 2 + (v % 2 + mask % 2) % 2


def encode(v):
    size = jnp.abs(v)
    s = jnp.maximum(jnp.max(size, axis=0, keepdims=True), 1e-30)
    s = (s * 1.004).astype(BF16).astype(F32)
    code = jnp.exp2(size * (SPAN / s) - SPAN / 2)
    return jnp.where(v < 0, -code, code).astype(BF16), s


def decode(code, s):
    code = code.astype(F32)
    size = jnp.log(jnp.abs(code)) * (s * (1.0 / (SPAN * math.log(2.0)))) + s * 0.5
    return jnp.where(code < 0, -size, size)


def kernel(
    group_tok, a_hbm, c_hbm, mom_hbm, left_hbm, left_t_hbm, right_hbm, right_t_hbm, up_hbm, new_hbm,
    a, c, ct, mom, left, left_t, right, right_t, pt, sent, received, ssc, rsc, up, new, band, bands,
    a_sem, in_sem, out_sem, sent_sem, rs, band_ss, band_rs,
):
    rep, own = lax.axis_index("rep"), lax.axis_index("fsdp")
    z0, y0, x0 = own // 16, own // 4 % 4, own % 4

    def partner(axis, mask):
        z, y, x = z0, y0, x0
        if axis == "x":
            x = flip(x, mask)
        elif axis == "y":
            y = flip(y, mask)
        else:
            z = flip(z, mask)
        return (rep, z * 16 + y * 4 + x)

    def slab(t):
        return (t + 1) % 2 * 2 + (t + 1) // 2 % 2

    def block_copy(t, ry):
        first = pl.multiple_of((flip(z0, slab(t)) * 16 + flip(y0, ry) * 4) * 128, 512)
        cols = pl.ds(first, 512)
        return pltpu.make_async_copy(a_hbm.at[:, cols], a.at[:, cols], a_sem.at[t, ry])

    barrier = pltpu.get_barrier_semaphore()
    others = [partner(axis, mask) for axis in "xyz" for mask in (1, 2, 3)]
    others += [((rep + i) % 4, own) for i in (1, 2, 3)]
    for other in others:
        pl.semaphore_signal(barrier, inc=1, device_id=other)
    pairs = [(c_hbm, c), (mom_hbm, mom), (left_hbm, left), (left_t_hbm, left_t), (right_hbm, right), (right_t_hbm, right_t)]
    inputs = [pltpu.make_async_copy(src, dst, in_sem.at[i]) for i, (src, dst) in enumerate(pairs)]
    inputs[0].start()
    for t in range(4):
        for ry in SLABS:
            block_copy(t, ry).start()
    for copy in inputs[1:]:
        copy.start()
    inputs[0].wait()
    ct[...] = c[...].T
    ssc[...] = jnp.zeros_like(ssc)

    def axis_of(f, p, stage):
        return ("zzxy", "zzyx")[p][stage] if f == 2 else ("xxyyzy", "yyxxzx")[f][stage]

    def mask_of(p, stage):
        return (FIRST[p][0], NEXT[p])[stage % 2]

    def begin(f, p, t, stage, row=0):
        at = FAMILIES[f] + p * STARTS[f][-1] + STARTS[f][stage] + t * SIZES[f][stage] + row
        return at if isinstance(at, int) else pl.multiple_of(at, 16)

    def message(f, p, t, stage, mask=None):
        where = pl.ds(begin(f, p, t, stage), SIZES[f][stage])
        return pltpu.make_async_remote_copy(
            sent.at[where], received.at[where], sent_sem.at[0], rs.at[f, p, t, stage],
            device_id=partner(axis_of(f, p, stage), mask or mask_of(p, stage)),
        )

    def put(f, p, t, stage, row, v):
        code, s = encode(v)
        sent[pl.ds(begin(f, p, t, stage, row * DEPTH[f]), DEPTH[f]), :] = code
        ssc[f, p, pl.ds(row, 1), :] = s

    def send(f, p, t, stage, mask=None):
        sent[pl.ds(begin(f, p, t, stage, UNITS[f][stage] * DEPTH[f]), 16), :] = ssc[f, p].astype(BF16)
        message(f, p, t, stage, mask).start()

    def receive(f, p, t, stage):
        message(f, p, t, stage).wait_recv()
        rsc[f, p] = received[pl.ds(begin(f, p, t, stage, UNITS[f][stage] * DEPTH[f]), 16), :].astype(F32)

    def got(f, p, t, stage, row):
        return decode(received[pl.ds(begin(f, p, t, stage, row * DEPTH[f]), DEPTH[f]), :], rsc[f, p, pl.ds(row, 1), :])

    def unit(f, p, t, sec, pri):
        at = (sec, pri) if f == 0 else (pri, sec)
        return (t,) + at + (slice((f * 2 + p) * 112, (f * 2 + p) * 112 + 112), slice(None))

    def multiply(t, ry):
        zh = flip(z0, slab(t))
        block_copy(t, ry).wait()
        parts = []
        for rx in range(4):
            col = (zh * 16 + flip(y0, ry) * 4 + flip(x0, rx)) * 128
            parts.append(a[:, pl.ds(pl.multiple_of(col, 128), 128)])
        total = jnp.dot(ct[...], jnp.concatenate(parts, axis=1), preferred_element_type=F32)
        for rx in range(4):
            pt[t, ry, rx] = total[:, rx * 128 : rx * 128 + 128]

    def z_unit(p, rz, ry, rx):
        return (SLABS.index(rz), ry, rx, slice(448 + p * 32, 480 + p * 32), slice(None))

    def products(t):
        for ry in SLABS:
            multiply(t, ry)

    def first(t):
        @pl.when(t == 0)
        def _():
            pl.semaphore_wait(barrier, len(others))

        for f, p in PORTIONS:
            for j, pri in enumerate(FIRST[p]):
                for sec in range(4):
                    put(f, p, t, 0, j * 4 + sec, pt[unit(f, p, t, sec, pri)])
            send(f, p, t, 0)

    def z_first():
        for p in range(2):

            def one(ry, carry):
                for j, rz in enumerate(FIRST[p]):
                    for rx in range(4):
                        put(2, p, ry, 0, j * 4 + rx, pt[z_unit(p, rz, ry, rx)])
                send(2, p, ry, 0)
                return carry

            lax.fori_loop(0, 4, one, 0)

    def z_second():
        for p in range(2):

            def one(ry, carry):
                receive(2, p, ry, 0)
                for rx in range(4):
                    put(2, p, ry, 1, rx, pt[z_unit(p, NEXT[p], ry, rx)] + got(2, p, ry, 0, 4 + rx))
                send(2, p, ry, 1)
                for rx in range(4):
                    pt[z_unit(p, 0, ry, rx)] += got(2, p, ry, 0, rx)
                return carry

            lax.fori_loop(0, 4, one, 0)

    def z_third():
        for p in range(2):

            def one(ry, carry):
                receive(2, p, ry, 1)
                for rx in range(4):
                    pt[z_unit(p, 0, ry, rx)] += got(2, p, ry, 1, rx)
                return carry

            lax.fori_loop(0, 4, one, 0)
            for m in (2, 1, 3):
                for other in range(4):
                    ry, rx = (other, m) if p == 0 else (m, other)
                    put(2, p, m - 1, 2, other, pt[z_unit(p, 0, ry, rx)])
                send(2, p, m - 1, 2, m)

    def z_fourth():
        for p in range(2):
            for m in (1, 3, 2):
                receive(2, p, m - 1, 2)
                for other in range(4):
                    ry, rx = (other, 0) if p == 0 else (0, other)
                    pt[z_unit(p, 0, ry, rx)] += got(2, p, m - 1, 2, other)
            for m in (2, 1, 3):
                ry, rx = (m, 0) if p == 0 else (0, m)
                put(2, p, m - 1, 3, 0, pt[z_unit(p, 0, ry, rx)])
                send(2, p, m - 1, 3, m)

    def z_last():
        for p in range(2):
            for m in (1, 3, 2):
                receive(2, p, m - 1, 3)
                pt[z_unit(p, 0, 0, 0)] += got(2, p, m - 1, 3, 0)

    def second(t):
        for f, p in PORTIONS:
            receive(f, p, t, 0)

            def pass_on(sec, carry):
                put(f, p, t, 1, sec, pt[unit(f, p, t, sec, NEXT[p])] + got(f, p, t, 0, 4 + sec))
                return carry

            lax.fori_loop(0, 4, pass_on, 0)
            send(f, p, t, 1)
        for f, p in PORTIONS:

            def keep(sec, carry):
                pt[unit(f, p, t, sec, 0)] += got(f, p, t, 0, sec)
                return carry

            lax.fori_loop(0, 4, keep, 0)

    def third_pairs(t):
        for f, p in PORTIONS:
            receive(f, p, t, 1)
            for j, sec in enumerate(FIRST[p]):
                put(f, p, t, 2, j, pt[unit(f, p, t, sec, 0)] + got(f, p, t, 1, sec))
            send(f, p, t, 2)
        for f, p in PORTIONS:
            for sec in (0, NEXT[p]):
                pt[unit(f, p, t, sec, 0)] += got(f, p, t, 1, sec)

    def third_direct(t):
        for f, p in PORTIONS:
            receive(f, p, t, 1)
            for m in (2, 1, 3):
                slot = (t - 2) * 3 + m - 1
                put(f, p, slot, 5, 0, pt[unit(f, p, t, m, 0)] + got(f, p, t, 1, m))
                send(f, p, slot, 5, m)
        for f, p in PORTIONS:
            pt[unit(f, p, t, 0, 0)] += got(f, p, t, 1, 0)

    def fourth_pairs(t):
        for f, p in PORTIONS:
            receive(f, p, t, 2)
            put(f, p, t, 3, 0, pt[unit(f, p, t, NEXT[p], 0)] + got(f, p, t, 2, 1))
            send(f, p, t, 3)
        for f, p in PORTIONS:
            pt[unit(f, p, t, 0, 0)] += got(f, p, t, 2, 0)

    def fourth_direct(t):
        for f, p in PORTIONS:
            v = pt[unit(f, p, t, 0, 0)]
            for m in (1, 3, 2):
                slot = (t - 2) * 3 + m - 1
                receive(f, p, slot, 5)
                v += got(f, p, slot, 5, 0)
            pt[unit(f, p, t, 0, 0)] = v

            @pl.when(t == 2)
            def _():
                put(f, p, 2, 4, 0, pt[unit(f, p, t, 0, 0)])
                send(f, p, 2, 4, 3)

    def fifth(t):
        for f, p in PORTIONS:
            receive(f, p, t, 3)
            pt[unit(f, p, t, 0, 0)] += got(f, p, t, 3, 0)
            for q in (2, 1):

                @pl.when(t == SLABS.index(q))
                def _():
                    put(f, p, q - 1, 4, 0, pt[unit(f, p, t, 0, 0)])
                    send(f, p, q - 1, 4, q)

    def last(q):
        for f, p in PORTIONS:
            receive(f, p, q - 1, 4)
            pt[unit(f, p, 3, 0, 0)] += got(f, p, q - 1, 4, 0)

    def at(when, stage, t):
        pl.when(when)(lambda: stage(t))

    def step(t, carry):
        at(t < 4, first, t)
        at(t < 3, products, t + 1)
        pl.when(t == 2)(z_first)
        at(jnp.logical_and(t >= 1, t < 5), second, t - 1)
        pl.when(t == 3)(z_second)
        pl.when(t == 5)(z_fourth)
        pl.when(t == 4)(z_third)
        at(jnp.logical_and(t >= 2, t < 4), third_pairs, t - 2)
        at(t >= 4, third_direct, t - 2)
        at(jnp.logical_and(t >= 3, t < 5), fourth_pairs, t - 3)
        at(t >= 5, fourth_direct, t - 3)
        at(t >= 4, fifth, t - 4)
        return carry

    products(0)
    lax.fori_loop(0, 6, step, 0)
    last(2)
    last(1)
    fourth_direct(3)
    z_last()
    last(3)
    for copy in inputs[1:]:
        copy.wait()

    def exact(l, r):
        return jnp.dot(l, r, preferred_element_type=F32, precision=lax.Precision.HIGHEST)

    accum = 0.9 * mom[0] + pt[3, 0, 0].T * (1.0 / math.sqrt(group_tok))
    mine = exact(exact(left[...], accum), right[...])
    band[...] = mine
    copies = [
        pltpu.make_async_remote_copy(
            band, bands.at[i - 1], band_ss.at[i - 1], band_rs.at[i - 1], device_id=((rep + i) % 4, own)
        )
        for i in (1, 2, 3)
    ]
    for copy in copies:
        copy.start()
    new[0] = accum - exact(exact(left_t[...], mine), right_t[...])
    outs = [pltpu.make_async_copy(*refs, out_sem.at[i]) for i, refs in enumerate(((up, up_hbm), (new, new_hbm)))]
    outs[1].start()
    for copy in copies:
        copy.wait_recv()
    mean = (mine + bands[0] + bands[1] + bands[2]) * 0.25
    up[...] = exact(exact(left_t[...], mean), right_t[...])
    outs[0].start()
    for copy in copies:
        copy.wait_send()
    pltpu.make_async_copy(sent, sent, sent_sem.at[0]).wait()
    for copy in outs:
        copy.wait()


def hand_on(up_ref, new_ref, up_out, new_out):
    up_out[...] = up_ref[...]
    new_out[...] = new_ref[...]


def shards(activations, cotangents, momentum):
    tok, d = activations.shape
    kw = cotangents.shape[1]
    basis = dct_basis()
    left = np.kron(np.eye(2, dtype=np.float32), basis)
    right = np.kron(np.eye(kw // 64, dtype=np.float32), basis.T)
    constants = [jnp.asarray(m) for m in (left, left.T.copy(), right, right.T.copy())]
    vmem = pl.BlockSpec(memory_space=pltpu.VMEM)
    hbm = pl.BlockSpec(memory_space=pl.ANY)
    dma = pltpu.SemaphoreType.DMA
    shapes = (jax.ShapeDtypeStruct((128, kw), F32), jax.ShapeDtypeStruct((1, 128, kw), F32))
    results = pl.pallas_call(
        functools.partial(kernel, tok * lax.axis_size("fsdp")),
        out_shape=shapes,
        in_specs=[hbm] * 7,
        out_specs=(hbm, hbm),
        scratch_shapes=[
            pltpu.VMEM((tok, d), BF16),
            pltpu.VMEM((tok, kw), BF16),
            pltpu.VMEM((kw, tok), BF16),
            pltpu.VMEM((1, 128, kw), F32),
            *[pltpu.VMEM(m.shape, F32) for m in constants],
            pltpu.VMEM((4, 4, 4, kw, 128), F32),
            pltpu.VMEM((FAMILIES[3], 128), BF16),
            pltpu.VMEM((FAMILIES[3], 128), BF16),
            pltpu.VMEM((3, 2, 16, 128), F32),
            pltpu.VMEM((3, 2, 16, 128), F32),
            *[pltpu.VMEM(m.shape, F32) for m in shapes],
            pltpu.VMEM((32, 128), F32),
            pltpu.VMEM((3, 32, 128), F32),
            dma((4, 4)),
            dma((6,)),
            dma((2,)),
            dma((1,)),
            dma((3, 2, 6, 6)),
            dma((3,)),
            dma((3,)),
        ],
        compiler_params=pltpu.CompilerParams(
            collective_id=0, has_side_effects=True, vmem_limit_bytes=60 * 2**20
        ),
        cost_estimate=pl.CostEstimate(flops=2 * tok * d * kw, bytes_accessed=2 * tok * (d + kw), transcendentals=0),
    )(activations, cotangents, momentum, *constants)
    return pl.pallas_call(
        hand_on,
        out_shape=shapes,
        in_specs=[vmem] * 2,
        out_specs=(vmem, vmem),
    )(*results)


def solution(mesh):
    return jax.shard_map(
        shards,
        mesh=mesh,
        in_specs=(P(("rep", "fsdp"), None), P(("rep", "fsdp"), None), P("rep", "fsdp", None)),
        out_specs=(P("fsdp", None), P("rep", "fsdp", None)),
        check_vma=False,
    )
```
